128 devices in a mesh: ta: 16 (over z_lo, y, core), xyz: 8 (over z_hi, x).
Axes of the slice: x: 4, y: 4, z: 4 (z_hi: 2, z_lo: 2; z = z_hi * 2 + z_lo), core: 2. Of those that a mesh axis runs over, the one named last changes fastest.
Arguments:
- fine_field: bfloat16 [16, 8, 16, 8, 2, 768], P('ta', None, 'xyz'), may hold values from -40 to 40
- null_vectors: bfloat16 [16, 8, 16, 8, 2, 32, 768], P('ta', None, 'xyz'), may hold values from -1 to 1
- coarse_links: bfloat16 [9, 32, 16, 8, 64, 128], P(None, 'ta', 'xyz'), may hold values from -0.35 to 19
Outputs:
- coarse_solution: float32 [32, 16, 8, 128], P('ta', 'xyz')
- coarse_residual: float32 [32, 16, 8, 128], P('ta', 'xyz')
The draws below stay inside these ranges and needn't reach their ends.
All inputs are finite; a program needn't handle non-finite values.
Results may differ from the reference program's by a relative error of at most 0.004.
Values may be sent and summed in bfloat16 or wider, within the bound.
No kernel may reach another device: no remote copies, remote signals or barrier semaphores. Data moves between devices by JAX's collectives and lax.ppermute only.
A program may use at most 64 MiB of HBM per device.

```python
import jax
import jax.numpy as jnp
from jax import lax

NVEC = 32
COARSE = 64
TSPAN = 4
FINE = 768
ITERS = 2
CY = 8
NT = 16
CT = 4
CX = 8
CZ = 16


def draw_fine_field(key, part):
    key = jax.random.fold_in(key, 11)
    key_values, key_scales, key_common, key_phase = jax.random.split(key, 4)
    extent = (NT, CX, CZ, CY, 2, FINE)
    values = jnp.clip(jax.random.normal(key_values, extent, jnp.float32), -5.0, 5.0)
    common = jnp.clip(jax.random.normal(key_common, (2, FINE), jnp.float32), -4.0, 4.0)
    row_scale = jnp.exp(jax.random.uniform(key_scales, extent[:5] + (1,), jnp.float32, -0.7, 0.7))
    phases = jax.random.uniform(key_phase, (4,), jnp.float32, 0.0, 6.2831853)
    turn = 6.2831853
    along_t = jnp.cos(turn * jnp.arange(NT, dtype=jnp.float32) / NT + phases[0])
    along_x = jnp.cos(turn * jnp.arange(CX, dtype=jnp.float32) / CX + phases[1])
    along_z = jnp.cos(turn * jnp.arange(CZ, dtype=jnp.float32) / CZ + phases[2])
    along_y = jnp.cos(turn * jnp.arange(CY, dtype=jnp.float32) / CY + phases[3])
    wave = 0.5 + 0.12 * (along_t[:, None, None, None] + along_x[None, :, None, None] + along_z[None, None, :, None] + along_y[None, None, None, :])
    mixed = 0.6 * values + 1.6 * common[None, None, None, None] * wave[:, :, :, :, None, None]
    time_ramp = jnp.arange(NT, dtype=jnp.float32) / (NT - 1) - 0.5
    depths = jnp.arange(CZ, dtype=jnp.float32) / max(CZ - 1, 1) - 0.5
    growth = jnp.exp(jnp.log(3.0) * (time_ramp[:, None, None, None, None, None] + depths[None, None, :, None, None, None]))
    return (mixed * row_scale * growth).astype(jnp.bfloat16)


def draw_null_vectors(key, part):
    key = jax.random.fold_in(key, 31)
    key_common, key_own = jax.random.split(key)
    extent = (NT, CX, CZ, CY, 2, NVEC, FINE)
    factor = (FINE * TSPAN) ** (-0.5)
    common = jnp.clip(jax.random.normal(key_common, (2, NVEC, FINE), jnp.float32), -4.0, 4.0)
    own = jnp.clip(jax.random.normal(key_own, extent, jnp.float32), -4.0, 4.0)
    return ((0.8 * common[None, None, None, None] + 0.6 * own) * factor).astype(jnp.bfloat16)


def draw_coarse_links(key, part):
    key = jax.random.fold_in(key, 23)
    key_noise, key_sites, key_hops = jax.random.split(key, 3)
    extent = (9, CX * CT, CZ, CY, COARSE, 2 * COARSE)
    noise = jnp.clip(jax.random.normal(key_noise, extent, jnp.float32), -4.0, 4.0)
    reach = jnp.log(8.0)
    hop_low = 0.08
    along_x = (jnp.arange(CX * CT) // CT).astype(jnp.float32) / (CX - 1)
    ramp = 1.5 * jnp.exp(reach * along_x)
    site_factor = jnp.exp(jax.random.uniform(key_sites, (CX * CT, CZ, CY), jnp.float32, -0.22, 0.22))
    level = (ramp[:, None, None] * site_factor)[None, :, :, :, None, None]
    hops = -jax.random.uniform(key_hops, (9, CX * CT, CZ, CY), jnp.float32, hop_low, 0.2)
    direction = jnp.arange(9)[:, None, None, None, None, None]
    spread = jnp.where(direction == 0, 0.06, 0.025)
    on_diagonal = (jnp.arange(COARSE)[:, None] == jnp.arange(2 * COARSE)[None, :])[None, None, None, None]
    diagonal = (on_diagonal & (direction == 0)).astype(jnp.float32)
    hop_diagonal = (on_diagonal & (direction > 0)).astype(jnp.float32)
    return (noise * spread + level * diagonal + hops[:, :, :, :, None, None] * hop_diagonal).astype(jnp.bfloat16)


def setup_inputs(seed: int = 0) -> dict:
    key_list = jax.random.split(jax.random.key(seed), 4)
    return {
        "fine_field": draw_fine_field(jax.random.fold_in(key_list[3], 71), 0),
        "null_vectors": draw_null_vectors(jax.random.fold_in(key_list[3], 71), 0),
        "coarse_links": draw_coarse_links(jax.random.fold_in(key_list[3], 71), 0),
    }


def rotated(values):
    pairs = values.reshape(values.shape[:-1] + (values.shape[-1] // 2, 2))
    turned = jnp.stack([pairs[..., 1], -pairs[..., 0]], axis=-1).reshape(values.shape)
    return jnp.stack([values, turned], axis=-2)


def complex_form(values):
    midpoint = values.shape[-1] // 2
    real_part = values[..., :midpoint]
    imag_part = values[..., midpoint:]
    return jnp.stack([jnp.concatenate([real_part, -imag_part], axis=-1),
                      jnp.concatenate([imag_part, real_part], axis=-1)], axis=-2)


def scaled(alpha_real, alpha_imag, values):
    midpoint = values.shape[-1] // 2
    real_part = values[..., :midpoint]
    imag_part = values[..., midpoint:]
    return jnp.concatenate([alpha_real * real_part - alpha_imag * imag_part,
                            alpha_real * imag_part + alpha_imag * real_part], axis=-1)


def restrict_slice(pieces):
    field, vectors = pieces
    turned = rotated(field).astype(jnp.float32)
    products = jnp.einsum('xzycof,xzyckf->xzyock', turned, vectors.astype(jnp.float32))
    return products.reshape(products.shape[:3] + (-1,))


def apply_coarse(vector, coarse_links):
    rounded = vector.astype(jnp.bfloat16)
    lattice = rounded.reshape((CX, CT, CZ, CY, 2 * COARSE))
    moves = ((0, 0), (0, -1), (0, 1), (3, -1), (3, 1), (2, -1), (2, 1), (1, -1), (1, 1))
    total = jnp.zeros((CX * CT, CZ, CY, 2, COARSE), jnp.float32)
    for direction, (axis_number, amount) in enumerate(moves):
        moved = jnp.roll(lattice, amount, axis=axis_number)
        forms = complex_form(moved.reshape((CX * CT, CZ, CY, 2 * COARSE))).astype(jnp.float32)
        total = total + jnp.einsum('rzyjm,rzyom->rzyoj', coarse_links[direction].astype(jnp.float32), forms)
    return total.reshape((CX * CT, CZ, CY, 2 * COARSE))


def reference(fine_field, null_vectors, coarse_links):
    partials = lax.map(restrict_slice, (fine_field, null_vectors))
    grouped = partials.reshape((CT, TSPAN, CX, CZ, CY, 2 * COARSE)).sum(axis=1)
    source = jnp.transpose(grouped, (1, 0, 2, 3, 4)).reshape((CX * CT, CZ, CY, 2 * COARSE))
    solution = jnp.zeros_like(source)
    residual = source
    for iteration in range(ITERS):
        image = apply_coarse(residual, coarse_links)
        image_real = image[..., :COARSE]
        image_imag = image[..., COARSE:]
        residual_real = residual[..., :COARSE]
        residual_imag = residual[..., COARSE:]
        dot_real = jnp.sum(image_real * residual_real + image_imag * residual_imag)
        dot_imag = jnp.sum(image_real * residual_imag - image_imag * residual_real)
        image_norm = jnp.sum(image_real * image_real + image_imag * image_imag)
        alpha_real = dot_real / image_norm
        alpha_imag = dot_imag / image_norm
        solution = solution + scaled(alpha_real, alpha_imag, residual)
        residual = residual - scaled(alpha_real, alpha_imag, image)
    return solution, residual
```

```python
import jax
import jax.numpy as jnp
from jax import lax
from jax.experimental import pallas as pl
from jax.experimental.pallas import tpu as pltpu
from jax.sharding import PartitionSpec as P

TSPAN = 4
HALF = 64
WIDE = 128
BF16 = jnp.bfloat16
F32 = jnp.float32
VMEM = pl.BlockSpec(memory_space=pltpu.VMEM)
LIMIT = 40 * 1024 * 1024


def iota(shape, dim):
    return lax.broadcasted_iota(jnp.int32, shape, dim)


def halves_swapped(values):
    return pltpu.roll(values, HALF, values.ndim - 1)


def own_site(products):
    folded = []
    row, lane = iota((8, WIDE), 0), iota((8, WIDE), 1)
    for o in range(2):
        total = jnp.zeros((8, WIDE), F32)
        for pair in range(4):
            block = products[o * 8 : o * 8 + 8, pair * WIDE : (pair + 1) * WIDE]
            total = total + jnp.where(row == 2 * pair + lane // HALF, block, 0.0)
        folded.append(total + halves_swapped(total))
    return jnp.where(lane < HALF, folded[0], folded[1])


def restrict_kernel(field_ref, vectors_ref, send_ref):
    x = pl.program_id(0)
    count = pl.num_programs(0)
    half = lax.axis_index("ta") // 8
    even = iota((16, 768), 1) % 2 == 0
    parts = []
    for z in range(2):
        values = field_ref[0, 0, z].astype(F32)
        values = jnp.concatenate([values[:, 0, :], values[:, 1, :]], axis=0)
        after = pltpu.roll(values, 767, 1)
        before = pltpu.roll(values, 1, 1)
        turned = jnp.where(even, after, -before)
        rows = jnp.concatenate([values, turned], axis=0).astype(BF16)
        vectors = vectors_ref[0, 0, z].reshape(512, 768)
        products = lax.dot_general(
            rows, vectors, (((1,), (1,)), ((), ())), preferred_element_type=F32
        )
        first = iota((8, 512), 1) // 32 % 2 == 0
        products = jnp.concatenate(
            [
                jnp.where(first, products[o * 16 : o * 16 + 8], products[o * 16 + 8 : o * 16 + 16])
                for o in range(2)
            ],
            axis=0,
        )
        parts.append(own_site(products))
    partial = jnp.stack(parts)
    high = partial.astype(BF16)
    low = (partial - high.astype(F32)).astype(BF16)
    behind = lax.rem(x + count - 1, count)
    ahead = lax.rem(x + 1, count)
    send_ref[2 * x + half, 0] = high
    send_ref[2 * x + half, 1] = low
    send_ref[2 * x + 1 - half, 0] = high
    send_ref[2 * x + 1 - half, 1] = low
    send_ref[2 * behind + half, 2] = high
    send_ref[2 * ahead + half, 3] = high
    send_ref[2 * x + 1 - half, 2] = high
    send_ref[2 * x + 1 - half, 3] = high


def gather_kernel(received_ref, source_ref, own_ref, other_ref, plus_ref, minus_ref):
    half = lax.axis_index("ta") % 2

    def summed(first, slots):
        rows = []
        for s in range(2):
            total = None
            for i in range(TSPAN):
                for slot in slots:
                    term = received_ref[first + s * TSPAN + i, slot].astype(F32)
                    total = term if total is None else total + term
            rows.append(total)
        return jnp.stack(rows)

    source = summed(8 * half, (0, 1))
    source_ref[...] = source
    own_ref[...] = source.astype(BF16)
    other_ref[...] = summed(8 - 8 * half, (0, 1)).astype(BF16)
    plus_ref[...] = summed(8 * half, (2,)).astype(BF16)
    minus_ref[...] = summed(8 * half, (3,)).astype(BF16)


def forms(v):
    lane = iota((8, WIDE), 1)
    return jnp.concatenate([jnp.where(lane < HALF, v, -v), halves_swapped(v)], axis=0).astype(BF16)


def applied(links_ref, own, other, plus, minus, up, down):
    rounded = own.astype(BF16).astype(F32)
    low = own - rounded
    plain, full = [], []
    for r in range(2):
        for z in range(2):
            here = rounded[r, z]
            neighbours = [
                here,
                plus[r, z],
                minus[r, z],
                pltpu.roll(here, 7, 0),
                pltpu.roll(here, 1, 0),
                rounded[r, 1] if z == 0 else up[r],
                down[r] if z == 0 else rounded[r, 0],
                rounded[1, z] if r == 0 else other[0, z],
                other[1, z] if r == 0 else rounded[0, z],
            ]
            matrices = [links_ref[d, r, z].reshape(512, WIDE) for d in range(9)]
            rows = [forms(v) for v in neighbours]
            total = lax.dot_general(
                jnp.concatenate([rows[0], forms(low[r, z])], axis=0),
                matrices[0],
                (((1,), (1,)), ((), ())),
                preferred_element_type=F32,
            )
            main = total[:16]
            for d in range(1, 9, 2):
                main = main + lax.dot_general(
                    jnp.concatenate(rows[d : d + 2], axis=1),
                    jnp.concatenate(matrices[d : d + 2], axis=1),
                    (((1,), (1,)), ((), ())),
                    preferred_element_type=F32,
                )
            value = own_site(main)
            plain.append(value)
            full.append(value + own_site(total[16:]))
    shape = (2, 2, 8, WIDE)
    return jnp.stack(plain).reshape(shape), jnp.stack(full).reshape(shape)


def first_kernel(links_ref, source_ref, other_ref, plus_ref, minus_ref, up_ref, down_ref, image_ref, full_ref, own_ref):
    image, full = applied(
        links_ref,
        source_ref[...],
        other_ref[...].astype(F32),
        plus_ref[...].astype(F32),
        minus_ref[...].astype(F32),
        up_ref[...].astype(F32),
        down_ref[...].astype(F32),
    )
    image_ref[...] = image
    full_ref[...] = full
    own_ref[...] = image.astype(BF16)


def turned_back(values):
    lane = iota(values.shape, values.ndim - 1)
    swapped = halves_swapped(values)
    return jnp.where(lane < HALF, swapped, -swapped)


def second_kernel(
    links_ref, source_ref, image_ref, full_ref, other_ref, plus_ref, minus_ref, up_ref, down_ref, twice_ref, sums_ref
):
    image = image_ref[...]
    _, twice = applied(
        links_ref,
        image,
        other_ref[...].astype(F32),
        plus_ref[...].astype(F32),
        minus_ref[...].astype(F32),
        up_ref[...].astype(F32),
        down_ref[...].astype(F32),
    )
    twice_ref[...] = twice
    source = source_ref[...]
    full = full_ref[...]
    rows = []

    def add(a, b):
        rows.append(jnp.sum((a * b).reshape(32, WIDE), axis=0, keepdims=True))

    def add_complex(a, b):
        add(a, b)
        add(a, turned_back(b))

    add_complex(image, source)
    add_complex(full, source)
    add_complex(full, image)
    add_complex(twice, source)
    add_complex(twice, image)
    add_complex(full, twice)
    add(image, image)
    add(full, full)
    add(twice, twice)
    rows.append(jnp.zeros((1, WIDE), F32))
    sums = jnp.sum(jnp.concatenate(rows, axis=0), axis=1, keepdims=True)
    line = jnp.sum(
        jnp.where(iota((16, WIDE), 0) == iota((16, WIDE), 1), sums, 0.0), axis=0, keepdims=True
    )
    sums_ref[...] = jnp.broadcast_to(line.reshape(1, 1, WIDE), sums_ref.shape)


def last_kernel(sums_ref, source_ref, image_ref, full_ref, twice_ref, solution_ref, residual_ref):
    line = jnp.sum(sums_ref[...], axis=0)

    def at(k):
        return line[:, k : k + 1]

    def times(a, b):
        return a[0] * b[0] - a[1] * b[1], a[0] * b[1] + a[1] * b[0]

    def pair(k):
        return at(2 * k), at(2 * k + 1)

    image_source, full_source, full_image, twice_source, twice_image, full_twice = (pair(k) for k in range(6))
    image_norm, full_norm, twice_norm = at(12), at(13), at(14)
    alpha = image_source[0] / image_norm, image_source[1] / image_norm
    conj = alpha[0], -alpha[1]
    size = alpha[0] * alpha[0] + alpha[1] * alpha[1]
    term_a = times(alpha, full_image)
    term_b = times(conj, twice_source)
    dot = (
        full_source[0] - term_a[0] - term_b[0] + size * twice_image[0],
        full_source[1] - term_a[1] - term_b[1] + size * twice_image[1],
    )
    norm = full_norm - 2.0 * times(alpha, full_twice)[0] + size * twice_norm
    beta = dot[0] / norm, dot[1] / norm

    def scaled(a, values):
        return a[0] * values - a[1] * turned_back(values)

    source = source_ref[...]
    residual = source - scaled(alpha, image_ref[...])
    second = full_ref[...] - scaled(alpha, twice_ref[...])
    solution_ref[...] = scaled(alpha, source) + scaled(beta, residual)
    residual_ref[...] = residual - scaled(beta, second)


def shift(block, axis, distance):
    count = lax.axis_size(axis)
    return lax.ppermute(block, axis, [(i, (i + distance) % count) for i in range(count)])


def from_core(block):
    return lax.ppermute(block, "ta", [(i, i ^ 1) for i in range(lax.axis_size("ta"))])


def struct(shape, dtype=F32):
    return jax.ShapeDtypeStruct(shape, dtype)


def params():
    return pltpu.CompilerParams(vmem_limit_bytes=LIMIT)


def halo(own):
    count_ta, count_xyz = lax.axis_size("ta"), lax.axis_size("xyz")
    other = from_core(own)
    odd = lax.axis_index("ta") % 2 == 1
    chip = jnp.concatenate([own, other], axis=0)
    along_x = lax.ppermute(
        chip, "ta", [(i, (i + (2 if i % 2 == 0 else -2)) % count_ta) for i in range(count_ta)]
    )
    along_z = lax.ppermute(
        jnp.where(odd, chip[:, 0], chip[:, 1]),
        ("ta", "xyz"),
        [
            (i * count_xyz + j, i * count_xyz + (j + (1 if i % 2 == 0 else -1)) % count_xyz)
            for i in range(count_ta)
            for j in range(count_xyz)
        ],
    )
    back = jnp.concatenate([along_x[2:], along_z[2:, None]], axis=1)
    swapped = from_core(back)
    mine = jnp.concatenate([along_x[:2], along_z[:2, None]], axis=1)
    plus = jnp.where(odd, mine, swapped)
    minus = jnp.where(odd, swapped, mine)
    return other, plus[:, :2], minus[:, :2], plus[:, 2], minus[:, 2]


def on_device(fine_field, null_vectors, coarse_links):
    field4 = (2, 2, 8, WIDE)
    send = pl.pallas_call(
        restrict_kernel,
        grid=(8,),
        in_specs=[
            pl.BlockSpec((1, 1, 2, 8, 2, 768), lambda x: (0, x, 0, 0, 0, 0)),
            pl.BlockSpec((1, 1, 2, 8, 2, 32, 768), lambda x: (0, x, 0, 0, 0, 0, 0)),
        ],
        out_specs=pl.BlockSpec((16, 4, 2, 8, WIDE), lambda x: (0, 0, 0, 0, 0)),
        out_shape=struct((16, 4, 2, 8, WIDE), BF16),
        compiler_params=params(),
        name="restrict",
    )(fine_field, null_vectors)
    received = lax.all_to_all(send, "ta", 0, 0)
    source, own, other, plus, minus = pl.pallas_call(
        gather_kernel,
        in_specs=[VMEM],
        out_specs=[VMEM] * 5,
        out_shape=[struct(field4)] + [struct(field4, BF16)] * 4,
        compiler_params=params(),
        name="gather",
    )(received)
    down = shift(own[:, 1], "xyz", 1)
    up = shift(own[:, 0], "xyz", -1)
    image, full, own = pl.pallas_call(
        first_kernel,
        in_specs=[VMEM] * 7,
        out_specs=[VMEM] * 3,
        out_shape=[struct(field4), struct(field4), struct(field4, BF16)],
        compiler_params=params(),
        name="first",
    )(coarse_links, source, other, plus, minus, up, down)
    twice, sums = pl.pallas_call(
        second_kernel,
        in_specs=[VMEM] * 9,
        out_specs=[VMEM] * 2,
        out_shape=[struct(field4), struct((128, 1, WIDE))],
        compiler_params=params(),
        name="second",
    )(coarse_links, source, image, full, *halo(own))
    sums = lax.all_to_all(sums, ("ta", "xyz"), 0, 0)
    return pl.pallas_call(
        last_kernel,
        in_specs=[VMEM] * 5,
        out_specs=[VMEM] * 2,
        out_shape=[struct(field4)] * 2,
        compiler_params=params(),
        name="last",
    )(sums, source, image, full, twice)


def solution(mesh):
    in_specs = (
        P("ta", None, "xyz", None, None, None),
        P("ta", None, "xyz", None, None, None, None),
        P(None, "ta", "xyz", None, None, None),
    )
    out_specs = (P("ta", "xyz", None, None), P("ta", "xyz", None, None))
    return jax.shard_map(
        on_device, mesh=mesh, in_specs=in_specs, out_specs=out_specs, check_vma=False
    )
```

```python
import jax
import jax.numpy as jnp
from jax import lax
from jax.experimental import pallas as pl
from jax.experimental.pallas import tpu as pltpu
from jax.sharding import PartitionSpec as P

TSPAN = 4
HALF = 64
WIDE = 128
BF16 = jnp.bfloat16
F32 = jnp.float32
VMEM = pl.BlockSpec(memory_space=pltpu.VMEM)
MIB = 1024 * 1024
STAGE = 2


def iota(shape, dim):
    return lax.broadcasted_iota(jnp.int32, shape, dim)


def halves_swapped(values):
    return pltpu.roll(values, HALF, values.ndim - 1)


def own_site(products):
    folded = []
    row, lane = iota((8, WIDE), 0), iota((8, WIDE), 1)
    for o in range(2):
        total = jnp.zeros((8, WIDE), F32)
        for pair in range(4):
            block = products[o * 8 : o * 8 + 8, pair * WIDE : (pair + 1) * WIDE]
            total = total + jnp.where(row == 2 * pair + lane // HALF, block, 0.0)
        folded.append(total + halves_swapped(total))
    return jnp.where(lane < HALF, folded[0], folded[1])


def restrict_kernel(
    field_hbm, vectors_hbm, links_hbm, send_ref, links_ref, field_ref, vectors_ref, field_sem, vectors_sem, links_sem
):
    half = lax.axis_index("ta") // 8
    count = field_ref.shape[0]
    copies = []
    for x in range(count):
        copies.append(pltpu.make_async_copy(field_hbm.at[0, x], field_ref.at[x], field_sem.at[x]))
        copies.append(pltpu.make_async_copy(vectors_hbm.at[0, x], vectors_ref.at[x], vectors_sem.at[x]))
    links_copy = pltpu.make_async_copy(links_hbm, links_ref, links_sem)
    for copy in copies + [links_copy]:
        copy.start()
    even = iota((16, 768), 1) % 2 == 0
    first = iota((8, 512), 1) // 32 % 2 == 0
    for x in range(count):
        if x % STAGE == 0:
            for copy in copies[2 * x : 2 * (x + STAGE)]:
                copy.wait()
        parts = []
        for z in range(2):
            values = field_ref[x, z].astype(F32)
            values = jnp.concatenate([values[:, 0, :], values[:, 1, :]], axis=0)
            turned = jnp.where(even, pltpu.roll(values, 767, 1), -pltpu.roll(values, 1, 1))
            products = lax.dot_general(
                jnp.concatenate([values, turned], axis=0).astype(BF16),
                vectors_ref[x, z].reshape(512, 768),
                (((1,), (1,)), ((), ())),
                preferred_element_type=F32,
            )
            products = [
                jnp.where(first, products[o * 16 : o * 16 + 8], products[o * 16 + 8 : o * 16 + 16])
                for o in range(2)
            ]
            parts.append(own_site(jnp.concatenate(products, axis=0)))
        partial = jnp.stack(parts)
        high = partial.astype(BF16)
        low = (partial - high.astype(F32)).astype(BF16)
        send_ref[2 * x + half, 0] = high
        send_ref[2 * x + half, 1] = low
        send_ref[2 * x + 1 - half, 0] = high
        send_ref[2 * x + 1 - half, 1] = low
        send_ref[2 * ((x - 1) % count) + half, 2] = high
        send_ref[2 * ((x + 1) % count) + half, 3] = high
        send_ref[2 * x + 1 - half, 2] = high
        send_ref[2 * x + 1 - half, 3] = high
    links_copy.wait()


def gather_kernel(received_ref, source_ref, edge_ref, other_ref, plus_ref, minus_ref):
    half = lax.axis_index("ta") % 2

    def summed(first, slots):
        rows = []
        for s in range(2):
            total = None
            for i in range(TSPAN):
                for slot in slots:
                    term = received_ref[first + s * TSPAN + i, slot].astype(F32)
                    total = term if total is None else total + term
            rows.append(total)
        return jnp.stack(rows)

    source = summed(8 * half, (0, 1))
    source_ref[...] = source
    other = summed(8 - 8 * half, (0, 1))
    other_ref[...] = other.astype(BF16)
    chip = jnp.concatenate([source, other], axis=0)
    edge_ref[...] = jnp.where(half == 1, chip[:, 0], chip[:, 1]).astype(BF16)
    plus_ref[...] = summed(8 * half, (2,)).astype(BF16)
    minus_ref[...] = summed(8 * half, (3,)).astype(BF16)


def forms(v):
    lane = iota((8, WIDE), 1)
    return jnp.concatenate([jnp.where(lane < HALF, v, -v), halves_swapped(v)], axis=0).astype(BF16)


def applied(links_ref, own, other, plus, minus, up, down):
    rounded = own.astype(BF16).astype(F32)
    low = own - rounded
    plain, full = [], []
    for r in range(2):
        for z in range(2):
            here = rounded[r, z]
            neighbours = [
                here,
                plus[r, z],
                minus[r, z],
                pltpu.roll(here, 7, 0),
                pltpu.roll(here, 1, 0),
                rounded[r, 1] if z == 0 else up[r],
                down[r] if z == 0 else rounded[r, 0],
                rounded[1, z] if r == 0 else other[0, z],
                other[1, z] if r == 0 else rounded[0, z],
            ]
            matrices = [links_ref[d, r, z].reshape(512, WIDE) for d in range(9)]
            rows = [forms(v) for v in neighbours]
            total = lax.dot_general(
                jnp.concatenate([rows[0], forms(low[r, z])], axis=0),
                matrices[0],
                (((1,), (1,)), ((), ())),
                preferred_element_type=F32,
            )
            main = total[:16]
            for d in range(1, 9, 2):
                main = main + lax.dot_general(
                    jnp.concatenate(rows[d : d + 2], axis=1),
                    jnp.concatenate(matrices[d : d + 2], axis=1),
                    (((1,), (1,)), ((), ())),
                    preferred_element_type=F32,
                )
            value = own_site(main)
            plain.append(value)
            full.append(value + own_site(total[16:]))
    shape = (2, 2, 8, WIDE)
    return jnp.stack(plain).reshape(shape), jnp.stack(full).reshape(shape)


def first_kernel(
    links_ref, source_ref, other_ref, plus_ref, minus_ref, along_z_ref, swapped_ref, image_ref, full_ref, own_ref, _
):
    up, down = ordered(along_z_ref[:2], swapped_ref[...])
    image, full = applied(
        links_ref,
        source_ref[...],
        other_ref[...].astype(F32),
        plus_ref[...].astype(F32),
        minus_ref[...].astype(F32),
        up,
        down,
    )
    image_ref[...] = image
    full_ref[...] = full
    own_ref[...] = image.astype(BF16)


def turned_back(values):
    lane = iota(values.shape, values.ndim - 1)
    swapped = halves_swapped(values)
    return jnp.where(lane < HALF, swapped, -swapped)


def second_kernel(
    links_ref, source_ref, image_ref, full_ref, other_ref, along_x_ref, along_z_ref, swapped_ref, twice_ref, sums_ref
):
    image = image_ref[...]
    plus, minus = ordered(along_x_ref[:2], swapped_ref[:, :2])
    up, down = ordered(along_z_ref[:2], swapped_ref[:, 2])
    _, twice = applied(
        links_ref,
        image,
        other_ref[...].astype(F32),
        plus,
        minus,
        up,
        down,
    )
    twice_ref[...] = twice
    source = source_ref[...]
    full = full_ref[...]
    rows = []

    def add(a, b):
        rows.append(jnp.sum((a * b).reshape(32, WIDE), axis=0, keepdims=True))

    def add_complex(a, b):
        add(a, b)
        add(a, turned_back(b))

    add_complex(image, source)
    add_complex(full, source)
    add_complex(full, image)
    add_complex(twice, source)
    add_complex(twice, image)
    add_complex(full, twice)
    add(image, image)
    add(full, full)
    add(twice, twice)
    rows.append(jnp.zeros((1, WIDE), F32))
    sums = jnp.sum(jnp.concatenate(rows, axis=0), axis=1, keepdims=True)
    line = jnp.sum(
        jnp.where(iota((16, WIDE), 0) == iota((16, WIDE), 1), sums, 0.0), axis=0, keepdims=True
    )
    sums_ref[...] = jnp.broadcast_to(line.reshape(1, 1, WIDE), sums_ref.shape)


def last_kernel(sums_ref, source_ref, image_ref, full_ref, twice_ref, solution_ref, residual_ref):
    line = jnp.sum(sums_ref[...], axis=0)

    def at(k):
        return line[:, k : k + 1]

    def times(a, b):
        return a[0] * b[0] - a[1] * b[1], a[0] * b[1] + a[1] * b[0]

    def pair(k):
        return at(2 * k), at(2 * k + 1)

    image_source, full_source, full_image, twice_source, twice_image, full_twice = (pair(k) for k in range(6))
    image_norm, full_norm, twice_norm = at(12), at(13), at(14)
    alpha = image_source[0] / image_norm, image_source[1] / image_norm
    conj = alpha[0], -alpha[1]
    size = alpha[0] * alpha[0] + alpha[1] * alpha[1]
    term_a = times(alpha, full_image)
    term_b = times(conj, twice_source)
    dot = (
        full_source[0] - term_a[0] - term_b[0] + size * twice_image[0],
        full_source[1] - term_a[1] - term_b[1] + size * twice_image[1],
    )
    norm = full_norm - 2.0 * times(alpha, full_twice)[0] + size * twice_norm
    beta = dot[0] / norm, dot[1] / norm

    def scaled(a, values):
        return a[0] * values - a[1] * turned_back(values)

    source = source_ref[...]
    residual = source - scaled(alpha, image_ref[...])
    second = full_ref[...] - scaled(alpha, twice_ref[...])
    solution_ref[...] = scaled(alpha, source) + scaled(beta, residual)
    residual_ref[...] = residual - scaled(beta, second)


def from_core(block):
    return lax.ppermute(block, "ta", [(i, i ^ 1) for i in range(lax.axis_size("ta"))])


def struct(shape, dtype=F32):
    return jax.ShapeDtypeStruct(shape, dtype)


def params(limit=16):
    return pltpu.CompilerParams(vmem_limit_bytes=limit * MIB)


def z_step(block):
    count_ta, count_xyz = lax.axis_size("ta"), lax.axis_size("xyz")
    route = [
        (i * count_xyz + j, i * count_xyz + (j + (1 if i % 2 == 0 else -1)) % count_xyz)
        for i in range(count_ta)
        for j in range(count_xyz)
    ]
    return lax.ppermute(block, ("ta", "xyz"), route)


def x_step(block):
    count = lax.axis_size("ta")
    return lax.ppermute(block, "ta", [(i, (i + (2 if i % 2 == 0 else -2)) % count) for i in range(count)])


def chip_kernel(_, own_ref, other_ref, links_ref, chip_ref, edge_ref):
    odd = lax.axis_index("ta") % 2 == 1
    chip_ref[:2] = own_ref[...]
    chip_ref[2:] = other_ref[...]
    edge_ref[...] = jnp.where(odd, chip_ref[:, 0].astype(F32), chip_ref[:, 1].astype(F32)).astype(BF16)


def swap_kernel(_, along_x_ref, along_z_ref, links_ref, back_ref):
    back_ref[:, :2] = along_x_ref[2:]
    back_ref[:, 2] = along_z_ref[2:]


def with_links(kernel, links, outs, *args):
    return pl.pallas_call(
        kernel,
        in_specs=[VMEM] * (1 + len(args)),
        out_specs=[VMEM] * (1 + len(outs)),
        out_shape=[pltpu.VMEM(links.shape, BF16)] + [struct(*out) for out in outs],
        input_output_aliases={0: 0},
        compiler_params=params(),
        name=kernel.__name__,
    )(links, *args)


def halo(own, links):
    other = from_core(own)
    links, chip, edge = with_links(chip_kernel, links, [((4, 2, 8, WIDE), BF16), ((4, 8, WIDE), BF16)], own, other)
    along_x, along_z = x_step(chip), z_step(edge)
    links, back = with_links(swap_kernel, links, [((2, 3, 8, WIDE), BF16)], along_x, along_z)
    return links, other, along_x, along_z, from_core(back)


def ordered(received, swapped):
    odd = lax.axis_index("ta") % 2 == 1
    received, swapped = received.astype(F32), swapped.astype(F32)
    return jnp.where(odd, received, swapped), jnp.where(odd, swapped, received)


def on_device(fine_field, null_vectors, coarse_links):
    field4 = (2, 2, 8, WIDE)
    send, links = pl.pallas_call(
        restrict_kernel,
        in_specs=[pl.BlockSpec(memory_space=pltpu.HBM)] * 3,
        out_specs=[VMEM] * 2,
        out_shape=[struct((16, 4, 2, 8, WIDE), BF16), pltpu.VMEM(coarse_links.shape, BF16)],
        scratch_shapes=[
            pltpu.VMEM(fine_field.shape[1:], BF16),
            pltpu.VMEM(null_vectors.shape[1:], BF16),
            pltpu.SemaphoreType.DMA((8,)),
            pltpu.SemaphoreType.DMA((8,)),
            pltpu.SemaphoreType.DMA,
        ],
        compiler_params=params(32),
        name="restrict",
    )(*(pltpu.with_memory_space_constraint(v, pltpu.HBM) for v in (fine_field, null_vectors, coarse_links)))
    received = lax.all_to_all(send, "ta", 0, 0)
    source, edge, other, plus, minus = pl.pallas_call(
        gather_kernel,
        in_specs=[VMEM],
        out_specs=[VMEM] * 5,
        out_shape=[struct(field4), struct((4, 8, WIDE), BF16)] + [struct(field4, BF16)] * 3,
        compiler_params=params(),
        name="gather",
    )(received)
    along_z = z_step(edge)
    swapped = from_core(along_z[2:])
    image, full, own, links = pl.pallas_call(
        first_kernel,
        in_specs=[VMEM] * 7,
        out_specs=[VMEM] * 4,
        out_shape=[struct(field4), struct(field4), struct(field4, BF16), pltpu.VMEM(links.shape, BF16)],
        input_output_aliases={0: 3},
        compiler_params=params(),
        name="first",
    )(links, source, other, plus, minus, along_z, swapped)
    links, *around = halo(own, links)
    twice, sums = pl.pallas_call(
        second_kernel,
        in_specs=[VMEM] * 8,
        out_specs=[VMEM] * 2,
        out_shape=[struct(field4), struct((128, 1, WIDE))],
        compiler_params=params(),
        name="second",
    )(pltpu.with_memory_space_constraint(links, pltpu.VMEM), source, image, full, *around)
    sums = lax.all_to_all(sums, ("ta", "xyz"), 0, 0)
    return pl.pallas_call(
        last_kernel,
        in_specs=[VMEM] * 5,
        out_specs=[VMEM] * 2,
        out_shape=[struct(field4)] * 2,
        compiler_params=params(),
        name="last",
    )(sums, source, image, full, twice)


def solution(mesh):
    in_specs = (
        P("ta", None, "xyz", None, None, None),
        P("ta", None, "xyz", None, None, None, None),
        P(None, "ta", "xyz", None, None, None),
    )
    out_specs = (P("ta", "xyz", None, None), P("ta", "xyz", None, None))
    return jax.shard_map(
        on_device, mesh=mesh, in_specs=in_specs, out_specs=out_specs, check_vma=False
    )
```

```python
import jax
import jax.numpy as jnp
from jax import lax
from jax.experimental import pallas as pl
from jax.experimental.pallas import tpu as pltpu
from jax.sharding import PartitionSpec as P

TSPAN = 4
HALF = 64
WIDE = 128
BF16 = jnp.bfloat16
F32 = jnp.float32
VMEM = pl.BlockSpec(memory_space=pltpu.VMEM)
MIB = 1024 * 1024
STAGE = 2
EDGE = 12


def iota(shape, dim):
    return lax.broadcasted_iota(jnp.int32, shape, dim)


def halves_swapped(values):
    return pltpu.roll(values, HALF, values.ndim - 1)


def own_site(products):
    folded = []
    row, lane = iota((8, WIDE), 0), iota((8, WIDE), 1)
    for o in range(2):
        total = jnp.zeros((8, WIDE), F32)
        for pair in range(4):
            block = products[o * 8 : o * 8 + 8, pair * WIDE : (pair + 1) * WIDE]
            total = total + jnp.where(row == 2 * pair + lane // HALF, block, 0.0)
        folded.append(total + halves_swapped(total))
    return jnp.where(lane < HALF, folded[0], folded[1])


def restrict_kernel(
    field_hbm, vectors_hbm, send_ref, field_ref, vectors_ref, products_ref, field_sem, vectors_sem
):
    count = field_ref.shape[0]
    copies = []
    for x in range(count):
        copies.append(pltpu.make_async_copy(field_hbm.at[0, x], field_ref.at[x], field_sem.at[x]))
        copies.append(pltpu.make_async_copy(vectors_hbm.at[0, x], vectors_ref.at[x], vectors_sem.at[x]))
    for copy in copies:
        copy.start()
    even = iota((16, 768), 1) % 2 == 0
    first = iota((8, 512), 1) // 32 % 2 == 0

    def multiply(x, z):
        values = field_ref[x, z].astype(F32)
        values = jnp.concatenate([values[:, 0, :], values[:, 1, :]], axis=0)
        turned = jnp.where(even, pltpu.roll(values, 767, 1), -pltpu.roll(values, 1, 1))
        products_ref[x, z] = lax.dot_general(
            jnp.concatenate([values, turned], axis=0).astype(BF16),
            vectors_ref[x, z].reshape(512, 768),
            (((1,), (1,)), ((), ())),
            preferred_element_type=F32,
        )

    def finish(x, z):
        products = products_ref[x, z]
        products = [
            jnp.where(first, products[o * 16 : o * 16 + 8], products[o * 16 + 8 : o * 16 + 16])
            for o in range(2)
        ]
        partial = own_site(jnp.concatenate(products, axis=0))
        send_ref[2 * x, z] = partial
        send_ref[2 * x + 1, z] = partial

    for stage in range(0, count + STAGE, STAGE):
        if stage < count:
            for copy in copies[2 * stage : 2 * (stage + STAGE)]:
                copy.wait()
        for x in range(stage, stage + STAGE):
            for z in range(2):
                if x < count:
                    multiply(x, z)
                if x >= STAGE:
                    finish(x - STAGE, z)


def edge_of(chip):
    plane = jnp.where(lax.axis_index("ta") % 2 == 1, chip[:, 0], chip[:, 1])
    return jnp.concatenate([plane, jnp.zeros((EDGE - 4,) + plane.shape[1:], F32)], axis=0).astype(BF16)


def gather_kernel(received_ref, source_ref, other_ref, chip_ref, edge_ref):
    half = lax.axis_index("ta") % 2

    def summed(first):
        rows = []
        for s in range(2):
            terms = [received_ref[first + s * TSPAN + i] for i in range(TSPAN)]
            rows.append((terms[0] + terms[1]) + (terms[2] + terms[3]))
        return jnp.stack(rows)

    source, other = summed(8 * half), summed(8 - 8 * half)
    chip = jnp.concatenate([source, other], axis=0)
    source_ref[...] = source
    other_ref[...] = other.astype(BF16)
    chip_ref[...] = chip.astype(BF16)
    edge_ref[...] = edge_of(chip)


def forms(v):
    lane = iota((8, WIDE), 1)
    return jnp.concatenate([jnp.where(lane < HALF, v, -v), halves_swapped(v)], axis=0).astype(BF16)


def hops(links_ref, r, z, terms):
    total = None
    for i in range(0, len(terms), 2):
        pair = terms[i : i + 2]
        product = lax.dot_general(
            jnp.concatenate([forms(v) for _, v in pair], axis=1),
            jnp.concatenate([links_ref[d, r, z].reshape(512, WIDE) for d, _ in pair], axis=1),
            (((1,), (1,)), ((), ())),
            preferred_element_type=F32,
        )
        total = product if total is None else total + product
    return total


def applied_here(links_ref, own, other, r):
    rounded = own.astype(BF16).astype(F32)
    low = own - rounded
    plain, lower = [], []
    for z in range(2):
        here = rounded[r, z]
        total = lax.dot_general(
            jnp.concatenate([forms(here), forms(low[r, z])], axis=0),
            links_ref[0, r, z].reshape(512, WIDE),
            (((1,), (1,)), ((), ())),
            preferred_element_type=F32,
        )
        terms = [
            (3, pltpu.roll(here, 7, 0)),
            (4, pltpu.roll(here, 1, 0)),
            (5, rounded[r, 1]) if z == 0 else (6, rounded[r, 0]),
            (7, rounded[1, z] if r == 0 else other[0, z]),
            (8, other[1, z] if r == 0 else rounded[0, z]),
        ]
        plain.append(own_site(total[:16] + hops(links_ref, r, z, terms)))
        lower.append(own_site(total[16:]))
    return jnp.stack(plain), jnp.stack(lower)


def applied_beyond(links_ref, along_x, step_x, along_z, step_z, edge, add):
    for r in range(2):
        for z, terms in (
            (edge, [(step_x, along_x(r, edge)), (step_z, along_z(r))]),
            (1 - edge, [(step_x, along_x(r, 1 - edge))]),
        ):
            add(r, z, own_site(hops(links_ref, r, z, [(d, v.astype(F32)) for d, v in terms])))


def first_here_kernel(links_hbm, source_ref, other_ref, links_ref, plain_ref, lower_ref, links_sem):
    copies = [
        [pltpu.make_async_copy(links_hbm.at[d, r], links_ref.at[d, r], links_sem.at[d, r]) for d in range(9)]
        for r in range(2)
    ]
    here = (0, 3, 4, 5, 6, 7, 8)
    for r in range(2):
        for d in here:
            copies[r][d].start()
    for r in range(2):
        for d in (1, 2):
            copies[r][d].start()
    source, other = source_ref[...], other_ref[...].astype(F32)
    for r in range(2):
        for d in here:
            copies[r][d].wait()
        plain_ref[r], lower_ref[r] = applied_here(links_ref, source, other, r)
    for r in range(2):
        for d in (1, 2):
            copies[r][d].wait()


def near_kernel(links_ref, here_ref, along_x_ref, along_z_ref, _, near_ref):
    odd = lax.axis_index("ta") % 2

    def add(r, z, value):
        near_ref[r, z] = here_ref[r, z] + value

    applied_beyond(
        links_ref, lambda r, z: along_x_ref[r, z], 2 - odd, lambda r: along_z_ref[r], 6 - odd, odd, add
    )


def far(links_ref, near_ref, swapped_ref, total_ref):
    odd = lax.axis_index("ta") % 2

    def add(r, z, value):
        total_ref[r, z] = near_ref[r, z] + value

    applied_beyond(
        links_ref, lambda r, z: swapped_ref[r, z], 1 + odd, lambda r: swapped_ref[r, 2], 5 + odd, 1 - odd, add
    )


def first_far_kernel(links_ref, near_ref, lower_ref, swapped_ref, _, image_ref, full_ref, own_ref):
    far(links_ref, near_ref, swapped_ref, image_ref)
    image = image_ref[...]
    full_ref[...] = image + lower_ref[...]
    own_ref[...] = image.astype(BF16)


def chip_kernel(_, own_ref, other_ref, links_ref, chip_ref, edge_ref):
    chip_ref[:2] = own_ref[...]
    chip_ref[2:] = other_ref[...]
    edge_ref[...] = edge_of(chip_ref[...].astype(F32))


def swap_kernel(_, along_x_ref, along_z_ref, links_ref, back_ref):
    back_ref[:, :2] = along_x_ref[2:]
    back_ref[:, 2] = along_z_ref[2:4]


def turned_back(values):
    lane = iota(values.shape, values.ndim - 1)
    swapped = halves_swapped(values)
    return jnp.where(lane < HALF, swapped, -swapped)


def sum_rows(pairs, norms):
    products = []
    for a, b in pairs:
        products += [a * b, a * turned_back(b)]
    products += [a * a for a in norms]
    return [jnp.sum(v.reshape(32, WIDE), axis=0, keepdims=True) for v in products]


def second_here_kernel(links_ref, image_ref, other_ref, source_ref, full_ref, _, here_ref, rows_ref):
    image, other = image_ref[...], other_ref[...].astype(F32)
    for r in range(2):
        plain, lower = applied_here(links_ref, image, other, r)
        here_ref[r] = plain + lower
    source, full = source_ref[...], full_ref[...]
    rows = sum_rows(((image, source), (full, source), (full, image)), (image, full))
    rows_ref[...] = jnp.concatenate(rows, axis=0)


def second_far_kernel(
    links_ref, near_ref, swapped_ref, source_ref, image_ref, full_ref, rows_ref, twice_ref, sums_ref
):
    far(links_ref, near_ref, swapped_ref, twice_ref)
    twice = twice_ref[...]
    rows = sum_rows(((twice, source_ref[...]), (twice, image_ref[...]), (full_ref[...], twice)), (twice,))
    rows = jnp.concatenate([rows_ref[...]] + rows + [jnp.zeros((1, WIDE), F32)], axis=0)
    sums = jnp.sum(rows, axis=1, keepdims=True)
    line = jnp.sum(
        jnp.where(iota((16, WIDE), 0) == iota((16, WIDE), 1), sums, 0.0), axis=0, keepdims=True
    )
    sums_ref[...] = jnp.broadcast_to(line.reshape(1, 1, WIDE), sums_ref.shape)


def last_kernel(sums_ref, source_ref, image_ref, full_ref, twice_ref, solution_ref, residual_ref):
    line = jnp.sum(jnp.sum(sums_ref[...].reshape(16, 8, WIDE), axis=0), axis=0, keepdims=True)

    def at(k):
        return jnp.broadcast_to(line[:, k : k + 1], (8, WIDE))

    def times(a, b):
        return a[0] * b[0] - a[1] * b[1], a[0] * b[1] + a[1] * b[0]

    image_source, full_source, full_image, twice_source, twice_image, full_twice = (
        (at(k), at(k + 1)) for k in (0, 2, 4, 8, 10, 12)
    )
    image_norm, full_norm, twice_norm = at(6), at(7), at(14)
    alpha = image_source[0] / image_norm, image_source[1] / image_norm
    conj = alpha[0], -alpha[1]
    size = alpha[0] * alpha[0] + alpha[1] * alpha[1]
    term_a = times(alpha, full_image)
    term_b = times(conj, twice_source)
    dot = (
        full_source[0] - term_a[0] - term_b[0] + size * twice_image[0],
        full_source[1] - term_a[1] - term_b[1] + size * twice_image[1],
    )
    norm = full_norm - 2.0 * times(alpha, full_twice)[0] + size * twice_norm
    beta = dot[0] / norm, dot[1] / norm

    def scaled(a, values):
        return a[0] * values - a[1] * turned_back(values)

    source = source_ref[...]
    residual = source - scaled(alpha, image_ref[...])
    second = full_ref[...] - scaled(alpha, twice_ref[...])
    solution_ref[...] = scaled(alpha, source) + scaled(beta, residual)
    residual_ref[...] = residual - scaled(beta, second)


def from_core(block):
    return lax.ppermute(block, "ta", [(i, i ^ 1) for i in range(lax.axis_size("ta"))])


def struct(shape, dtype=F32):
    return jax.ShapeDtypeStruct(shape, dtype)


def z_step(block):
    count_ta, count_xyz = lax.axis_size("ta"), lax.axis_size("xyz")
    route = [
        (i * count_xyz + j, i * count_xyz + (j + (1 if i % 2 == 0 else -1)) % count_xyz)
        for i in range(count_ta)
        for j in range(count_xyz)
    ]
    return lax.ppermute(block, ("ta", "xyz"), route)


def x_step(block):
    count = lax.axis_size("ta")
    return lax.ppermute(block, "ta", [(i, (i + (2 if i % 2 == 0 else -2)) % count) for i in range(count)])


def call(kernel, outs, *args, limit=16, aliases=(), scratch=(), specs=None):
    return pl.pallas_call(
        kernel,
        in_specs=specs or [VMEM] * len(args),
        out_specs=[VMEM] * len(outs),
        out_shape=outs,
        input_output_aliases=dict(aliases),
        scratch_shapes=scratch,
        compiler_params=pltpu.CompilerParams(vmem_limit_bytes=limit * MIB),
        name=kernel.__name__,
    )(*args)


def in_hbm(array):
    return pltpu.with_memory_space_constraint(array, pltpu.HBM)


def on_device(fine_field, null_vectors, coarse_links):
    hbm = pl.BlockSpec(memory_space=pltpu.HBM)
    site = (2, 2, 8, WIDE)
    field, coarse = struct(site), struct(site, BF16)
    chip_rows, edge_rows = struct((4, 2, 8, WIDE), BF16), struct((EDGE, 8, WIDE), BF16)
    back_rows = struct((2, 3, 8, WIDE), BF16)
    held = pltpu.VMEM(coarse_links.shape, BF16)
    through = ((0, 0),)

    (send,) = call(
        restrict_kernel,
        [struct((16, 2, 8, WIDE))],
        in_hbm(fine_field),
        in_hbm(null_vectors),
        limit=32,
        specs=[hbm] * 2,
        scratch=[
            pltpu.VMEM(fine_field.shape[1:], BF16),
            pltpu.VMEM(null_vectors.shape[1:], BF16),
            pltpu.VMEM((8, 2, 32, 512), F32),
            pltpu.SemaphoreType.DMA((8,)),
            pltpu.SemaphoreType.DMA((8,)),
        ],
    )
    received = lax.all_to_all(send, "ta", 0, 0)
    source, other, chip, edge = call(gather_kernel, [field, coarse, chip_rows, edge_rows], received)

    along_x, along_z = x_step(chip), z_step(edge)
    links, plain, lower = call(
        first_here_kernel,
        [held, field, field],
        in_hbm(coarse_links),
        source,
        other,
        specs=[hbm, VMEM, VMEM],
        scratch=[pltpu.SemaphoreType.DMA((9, 2))],
    )
    links, back = call(swap_kernel, [held, back_rows], links, along_x, along_z, aliases=through)
    swapped = from_core(back)
    links, near = call(near_kernel, [held, field], links, plain, along_x, along_z, aliases=through)
    links, image, full, own = call(
        first_far_kernel, [held, field, field, coarse], links, near, lower, swapped, aliases=through
    )

    other = from_core(own)
    links, chip, edge = call(chip_kernel, [held, chip_rows, edge_rows], links, own, other, aliases=through)
    along_x, along_z = x_step(chip), z_step(edge)
    links, here, rows = call(
        second_here_kernel, [held, field, struct((8, WIDE))], links, image, other, source, full, aliases=through
    )
    links, back = call(swap_kernel, [held, back_rows], links, along_x, along_z, aliases=through)
    swapped = from_core(back)
    links, near = call(near_kernel, [held, field], links, here, along_x, along_z, aliases=through)
    twice, sums = call(
        second_far_kernel,
        [field, struct((128, 1, WIDE))],
        links,
        near,
        swapped,
        source,
        image,
        full,
        rows,
    )
    sums = lax.all_to_all(sums, ("ta", "xyz"), 0, 0)
    return call(last_kernel, [field, field], sums, source, image, full, twice)


def solution(mesh):
    in_specs = (
        P("ta", None, "xyz", None, None, None),
        P("ta", None, "xyz", None, None, None, None),
        P(None, "ta", "xyz", None, None, None),
    )
    out_specs = (P("ta", "xyz", None, None), P("ta", "xyz", None, None))
    return jax.shard_map(
        on_device, mesh=mesh, in_specs=in_specs, out_specs=out_specs, check_vma=False
    )
```

```python
import jax
import jax.numpy as jnp
from jax import lax
from jax.experimental import pallas as pl
from jax.experimental.pallas import tpu as pltpu
from jax.sharding import PartitionSpec as P

TSPAN = 4
HALF = 64
WIDE = 128
BF16 = jnp.bfloat16
F32 = jnp.float32
VMEM = pl.BlockSpec(memory_space=pltpu.VMEM)
MIB = 1024 * 1024
STAGE = 2
EDGE = 12


def iota(shape, dim):
    return lax.broadcasted_iota(jnp.int32, shape, dim)


def halves_swapped(values):
    return pltpu.roll(values, HALF, values.ndim - 1)


def own_site(products):
    folded = []
    row, lane = iota((8, WIDE), 0), iota((8, WIDE), 1)
    for o in range(2):
        total = jnp.zeros((8, WIDE), F32)
        for pair in range(4):
            block = products[o * 8 : o * 8 + 8, pair * WIDE : (pair + 1) * WIDE]
            total = total + jnp.where(row == 2 * pair + lane // HALF, block, 0.0)
        folded.append(total + halves_swapped(total))
    return jnp.where(lane < HALF, folded[0], folded[1])


def restrict_kernel(
    field_hbm, vectors_hbm, send_ref, field_ref, vectors_ref, products_ref, field_sem, vectors_sem
):
    count = field_ref.shape[0]
    copies = []
    for x in range(count):
        copies.append(pltpu.make_async_copy(field_hbm.at[0, x], field_ref.at[x], field_sem.at[x]))
        copies.append(pltpu.make_async_copy(vectors_hbm.at[0, x], vectors_ref.at[x], vectors_sem.at[x]))
    for copy in copies:
        copy.start()
    even = iota((16, 768), 1) % 2 == 0
    first = iota((8, 512), 1) // 32 % 2 == 0

    def multiply(x, z):
        values = field_ref[x, z].astype(F32)
        values = jnp.concatenate([values[:, 0, :], values[:, 1, :]], axis=0)
        turned = jnp.where(even, pltpu.roll(values, 767, 1), -pltpu.roll(values, 1, 1))
        products_ref[x, z] = lax.dot_general(
            jnp.concatenate([values, turned], axis=0).astype(BF16),
            vectors_ref[x, z].reshape(512, 768),
            (((1,), (1,)), ((), ())),
            preferred_element_type=F32,
        )

    def finish(x, z):
        products = products_ref[x, z]
        products = [
            jnp.where(first, products[o * 16 : o * 16 + 8], products[o * 16 + 8 : o * 16 + 16])
            for o in range(2)
        ]
        partial = own_site(jnp.concatenate(products, axis=0))
        send_ref[2 * x, z] = partial
        send_ref[2 * x + 1, z] = partial

    for stage in range(0, count + STAGE, STAGE):
        if stage < count:
            for copy in copies[2 * stage : 2 * (stage + STAGE)]:
                copy.wait()
        for x in range(stage, stage + STAGE):
            for z in range(2):
                if x < count:
                    multiply(x, z)
                if x >= STAGE:
                    finish(x - STAGE, z)


def edge_of(chip):
    return jnp.where(lax.axis_index("ta") % 2 == 1, chip[:, 0], chip[:, 1]).astype(BF16)


def gather_kernel(received_ref, source_ref, other_ref, chip_ref, edge_ref):
    half = lax.axis_index("ta") % 2

    def summed(first):
        rows = []
        for s in range(2):
            terms = [received_ref[first + s * TSPAN + i] for i in range(TSPAN)]
            rows.append((terms[0] + terms[1]) + (terms[2] + terms[3]))
        return jnp.stack(rows)

    source, other = summed(8 * half), summed(8 - 8 * half)
    chip = jnp.concatenate([source, other], axis=0)
    source_ref[...] = source
    other_ref[...] = other.astype(BF16)
    chip_ref[...] = chip.astype(BF16)
    edge_ref[...] = edge_of(chip)


def forms(v):
    lane = iota((8, WIDE), 1)
    return jnp.concatenate([jnp.where(lane < HALF, v, -v), halves_swapped(v)], axis=0).astype(BF16)


def hops(links_ref, r, z, terms):
    total = None
    for i in range(0, len(terms), 2):
        pair = terms[i : i + 2]
        product = lax.dot_general(
            jnp.concatenate([forms(v) for _, v in pair], axis=1),
            jnp.concatenate([links_ref[d, r, z].reshape(512, WIDE) for d, _ in pair], axis=1),
            (((1,), (1,)), ((), ())),
            preferred_element_type=F32,
        )
        total = product if total is None else total + product
    return total


def applied_here(links_ref, own, other, r):
    rounded = own.astype(BF16).astype(F32)
    low = own - rounded
    plain, lower = [], []
    for z in range(2):
        here = rounded[r, z]
        total = lax.dot_general(
            jnp.concatenate([forms(here), forms(low[r, z])], axis=0),
            links_ref[0, r, z].reshape(512, WIDE),
            (((1,), (1,)), ((), ())),
            preferred_element_type=F32,
        )
        terms = [
            (3, pltpu.roll(here, 7, 0)),
            (4, pltpu.roll(here, 1, 0)),
            (5, rounded[r, 1]) if z == 0 else (6, rounded[r, 0]),
            (7, rounded[1, z] if r == 0 else other[0, z]),
            (8, other[1, z] if r == 0 else rounded[0, z]),
        ]
        plain.append(own_site(total[:16] + hops(links_ref, r, z, terms)))
        lower.append(own_site(total[16:]))
    return jnp.stack(plain), jnp.stack(lower)


def applied_beyond(links_ref, along_x, step_x, along_z, step_z, edge, add):
    for r in range(2):
        for z, terms in (
            (edge, [(step_x, along_x(r, edge)), (step_z, along_z(r))]),
            (1 - edge, [(step_x, along_x(r, 1 - edge))]),
        ):
            add(r, z, own_site(hops(links_ref, r, z, [(d, v.astype(F32)) for d, v in terms])))


def first_here_kernel(links_hbm, source_ref, other_ref, links_ref, plain_ref, lower_ref, links_sem):
    copies = [
        [pltpu.make_async_copy(links_hbm.at[d, r], links_ref.at[d, r], links_sem.at[d, r]) for d in range(9)]
        for r in range(2)
    ]
    here = (0, 3, 4, 5, 6, 7, 8)
    for r in range(2):
        for d in here:
            copies[r][d].start()
    for r in range(2):
        for d in (1, 2):
            copies[r][d].start()
    source, other = source_ref[...], other_ref[...].astype(F32)
    for r in range(2):
        for d in here:
            copies[r][d].wait()
        plain_ref[r], lower_ref[r] = applied_here(links_ref, source, other, r)
    for r in range(2):
        for d in (1, 2):
            copies[r][d].wait()


def near_kernel(links_ref, here_ref, along_x_ref, along_z_ref, _, near_ref):
    odd = lax.axis_index("ta") % 2

    def add(r, z, value):
        near_ref[r, z] = here_ref[r, z] + value

    applied_beyond(
        links_ref, lambda r, z: along_x_ref[r, z], 2 - odd, lambda r: along_z_ref[r], 6 - odd, odd, add
    )


def far(links_ref, near_ref, swapped_ref, total_ref):
    odd = lax.axis_index("ta") % 2

    def add(r, z, value):
        total_ref[r, z] = near_ref[r, z] + value

    applied_beyond(
        links_ref, lambda r, z: swapped_ref[r, z], 1 + odd, lambda r: swapped_ref[r, 2], 5 + odd, 1 - odd, add
    )


def first_far_kernel(links_ref, near_ref, lower_ref, swapped_ref, _, image_ref, full_ref, own_ref):
    far(links_ref, near_ref, swapped_ref, image_ref)
    image = image_ref[...]
    full_ref[...] = image + lower_ref[...]
    own_ref[...] = image.astype(BF16)


def chip_kernel(_, own_ref, other_ref, links_ref, chip_ref, edge_ref):
    chip_ref[:2] = own_ref[...]
    chip_ref[2:] = other_ref[...]
    edge_ref[:4] = edge_of(chip_ref[...].astype(F32))
    edge_ref[4:] = jnp.zeros((EDGE - 4, 8, WIDE), BF16)


def swap_kernel(_, along_x_ref, along_z_ref, links_ref, back_ref):
    back_ref[:, :2] = along_x_ref[2:]
    back_ref[:, 2] = along_z_ref[2:4]


def turned_back(values):
    lane = iota(values.shape, values.ndim - 1)
    swapped = halves_swapped(values)
    return jnp.where(lane < HALF, swapped, -swapped)


def sum_rows(pairs, norms):
    products = []
    for a, b in pairs:
        products += [a * b, a * turned_back(b)]
    products += [a * a for a in norms]
    return [jnp.sum(v.reshape(32, WIDE), axis=0, keepdims=True) for v in products]


def second_here_kernel(links_ref, image_ref, other_ref, source_ref, full_ref, _, here_ref, rows_ref):
    image, other = image_ref[...], other_ref[...].astype(F32)
    for r in range(2):
        plain, lower = applied_here(links_ref, image, other, r)
        here_ref[r] = plain + lower
    source, full = source_ref[...], full_ref[...]
    rows = sum_rows(((image, source), (full, source), (full, image)), (image, full))
    rows_ref[...] = jnp.concatenate(rows, axis=0)


def second_far_kernel(
    links_ref, near_ref, swapped_ref, source_ref, image_ref, full_ref, rows_ref, twice_ref, sums_ref
):
    far(links_ref, near_ref, swapped_ref, twice_ref)
    twice = twice_ref[...]
    rows = sum_rows(((twice, source_ref[...]), (twice, image_ref[...]), (full_ref[...], twice)), (twice,))
    rows = jnp.concatenate([rows_ref[...]] + rows + [jnp.zeros((1, WIDE), F32)], axis=0)
    sums = jnp.sum(rows, axis=1, keepdims=True)
    line = jnp.sum(
        jnp.where(iota((16, WIDE), 0) == iota((16, WIDE), 1), sums, 0.0), axis=0, keepdims=True
    )
    sums_ref[...] = jnp.broadcast_to(line.reshape(1, 1, WIDE), sums_ref.shape)


def last_kernel(sums_ref, source_ref, image_ref, full_ref, twice_ref, solution_ref, residual_ref):
    line = jnp.sum(jnp.sum(sums_ref[...].reshape(16, 8, WIDE), axis=0), axis=0, keepdims=True)

    def at(k):
        return jnp.broadcast_to(line[:, k : k + 1], (8, WIDE))

    def times(a, b):
        return a[0] * b[0] - a[1] * b[1], a[0] * b[1] + a[1] * b[0]

    image_source, full_source, full_image, twice_source, twice_image, full_twice = (
        (at(k), at(k + 1)) for k in (0, 2, 4, 8, 10, 12)
    )
    image_norm, full_norm, twice_norm = at(6), at(7), at(14)
    alpha = image_source[0] / image_norm, image_source[1] / image_norm
    conj = alpha[0], -alpha[1]
    size = alpha[0] * alpha[0] + alpha[1] * alpha[1]
    term_a = times(alpha, full_image)
    term_b = times(conj, twice_source)
    dot = (
        full_source[0] - term_a[0] - term_b[0] + size * twice_image[0],
        full_source[1] - term_a[1] - term_b[1] + size * twice_image[1],
    )
    norm = full_norm - 2.0 * times(alpha, full_twice)[0] + size * twice_norm
    beta = dot[0] / norm, dot[1] / norm

    def scaled(a, values):
        return a[0] * values - a[1] * turned_back(values)

    source = source_ref[...]
    residual = source - scaled(alpha, image_ref[...])
    second = full_ref[...] - scaled(alpha, twice_ref[...])
    solution_ref[...] = scaled(alpha, source) + scaled(beta, residual)
    residual_ref[...] = residual - scaled(beta, second)


def from_core(block):
    return lax.ppermute(block, "ta", [(i, i ^ 1) for i in range(lax.axis_size("ta"))])


def struct(shape, dtype=F32):
    return jax.ShapeDtypeStruct(shape, dtype)


def z_step(block):
    count_ta, count_xyz = lax.axis_size("ta"), lax.axis_size("xyz")
    route = [
        (i * count_xyz + j, i * count_xyz + (j + (1 if i % 2 == 0 else -1)) % count_xyz)
        for i in range(count_ta)
        for j in range(count_xyz)
    ]
    return lax.ppermute(block, ("ta", "xyz"), route)


def x_step(block):
    count = lax.axis_size("ta")
    return lax.ppermute(block, "ta", [(i, (i + (2 if i % 2 == 0 else -2)) % count) for i in range(count)])


def call(kernel, outs, *args, limit=16, aliases=(), scratch=(), specs=None):
    return pl.pallas_call(
        kernel,
        in_specs=specs or [VMEM] * len(args),
        out_specs=[VMEM] * len(outs),
        out_shape=outs,
        input_output_aliases=dict(aliases),
        scratch_shapes=scratch,
        compiler_params=pltpu.CompilerParams(vmem_limit_bytes=limit * MIB),
        name=kernel.__name__,
    )(*args)


def in_hbm(array):
    return pltpu.with_memory_space_constraint(array, pltpu.HBM)


def on_device(fine_field, null_vectors, coarse_links):
    hbm = pl.BlockSpec(memory_space=pltpu.HBM)
    site = (2, 2, 8, WIDE)
    field, coarse = struct(site), struct(site, BF16)
    chip_rows, edge_rows = struct((4, 2, 8, WIDE), BF16), struct((4, 8, WIDE), BF16)
    back_rows = struct((2, 3, 8, WIDE), BF16)
    held = pltpu.VMEM(coarse_links.shape, BF16)
    through = ((0, 0),)

    (send,) = call(
        restrict_kernel,
        [struct((16, 2, 8, WIDE))],
        in_hbm(fine_field),
        in_hbm(null_vectors),
        limit=32,
        specs=[hbm] * 2,
        scratch=[
            pltpu.VMEM(fine_field.shape[1:], BF16),
            pltpu.VMEM(null_vectors.shape[1:], BF16),
            pltpu.VMEM((8, 2, 32, 512), F32),
            pltpu.SemaphoreType.DMA((8,)),
            pltpu.SemaphoreType.DMA((8,)),
        ],
    )
    received = lax.all_to_all(send, "ta", 0, 0)
    source, other, chip, edge = call(gather_kernel, [field, coarse, chip_rows, edge_rows], received)

    along_x, along_z = x_step(chip), z_step(edge)
    links, plain, lower = call(
        first_here_kernel,
        [held, field, field],
        in_hbm(coarse_links),
        source,
        other,
        specs=[hbm, VMEM, VMEM],
        scratch=[pltpu.SemaphoreType.DMA((9, 2))],
    )
    links, back = call(swap_kernel, [held, back_rows], links, along_x, along_z, aliases=through)
    swapped = from_core(back)
    links, near = call(near_kernel, [held, field], links, plain, along_x, along_z, aliases=through)
    links, image, full, own = call(
        first_far_kernel, [held, field, field, coarse], links, near, lower, swapped, aliases=through
    )

    other = from_core(own)
    links, chip, edge = call(chip_kernel, [held, chip_rows, struct((EDGE, 8, WIDE), BF16)], links, own, other, aliases=through)
    along_x, along_z = x_step(chip), z_step(edge)
    links, here, rows = call(
        second_here_kernel, [held, field, struct((8, WIDE))], links, image, other, source, full, aliases=through
    )
    links, back = call(swap_kernel, [held, back_rows], links, along_x, along_z, aliases=through)
    swapped = from_core(back)
    links, near = call(near_kernel, [held, field], links, here, along_x, along_z, aliases=through)
    twice, sums = call(
        second_far_kernel,
        [field, struct((128, 1, WIDE))],
        links,
        near,
        swapped,
        source,
        image,
        full,
        rows,
    )
    sums = lax.all_to_all(sums, ("ta", "xyz"), 0, 0)
    return call(last_kernel, [field, field], sums, source, image, full, twice)


def solution(mesh):
    in_specs = (
        P("ta", None, "xyz", None, None, None),
        P("ta", None, "xyz", None, None, None, None),
        P(None, "ta", "xyz", None, None, None),
    )
    out_specs = (P("ta", "xyz", None, None), P("ta", "xyz", None, None))
    return jax.shard_map(
        on_device, mesh=mesh, in_specs=in_specs, out_specs=out_specs, check_vma=False
    )
```

```python
import jax
import jax.numpy as jnp
from jax import lax
from jax.experimental import pallas as pl
from jax.experimental.pallas import tpu as pltpu
from jax.sharding import PartitionSpec as P

TSPAN = 4
HALF = 64
WIDE = 128
BF16 = jnp.bfloat16
F32 = jnp.float32
VMEM = pl.BlockSpec(memory_space=pltpu.VMEM)
MIB = 1024 * 1024
STAGE = 2
EDGE = 12


def iota(shape, dim):
    return lax.broadcasted_iota(jnp.int32, shape, dim)


def halves_swapped(values):
    return pltpu.roll(values, HALF, values.ndim - 1)


def own_site(products):
    folded = []
    row, lane = iota((8, WIDE), 0), iota((8, WIDE), 1)
    for o in range(2):
        total = jnp.zeros((8, WIDE), F32)
        for pair in range(4):
            block = products[o * 8 : o * 8 + 8, pair * WIDE : (pair + 1) * WIDE]
            total = total + jnp.where(row == 2 * pair + lane // HALF, block, 0.0)
        folded.append(total + halves_swapped(total))
    return jnp.where(lane < HALF, folded[0], folded[1])


def restrict_kernel(
    field_hbm, vectors_hbm, send_ref, field_ref, vectors_ref, products_ref, field_sem, vectors_sem
):
    count = field_ref.shape[0]
    copies = []
    for x in range(count):
        copies.append(pltpu.make_async_copy(field_hbm.at[0, x], field_ref.at[x], field_sem.at[x]))
        copies.append(pltpu.make_async_copy(vectors_hbm.at[0, x], vectors_ref.at[x], vectors_sem.at[x]))
    for copy in copies:
        copy.start()
    even = iota((16, 768), 1) % 2 == 0
    first = iota((8, 512), 1) // 32 % 2 == 0

    def multiply(x, z):
        values = field_ref[x, z].astype(F32)
        values = jnp.concatenate([values[:, 0, :], values[:, 1, :]], axis=0)
        turned = jnp.where(even, pltpu.roll(values, 767, 1), -pltpu.roll(values, 1, 1))
        products_ref[x, z] = lax.dot_general(
            jnp.concatenate([values, turned], axis=0).astype(BF16),
            vectors_ref[x, z].reshape(512, 768),
            (((1,), (1,)), ((), ())),
            preferred_element_type=F32,
        )

    def finish(x, z):
        products = products_ref[x, z]
        products = [
            jnp.where(first, products[o * 16 : o * 16 + 8], products[o * 16 + 8 : o * 16 + 16])
            for o in range(2)
        ]
        partial = own_site(jnp.concatenate(products, axis=0))
        send_ref[2 * x, z] = partial
        send_ref[2 * x + 1, z] = partial

    for stage in range(0, count + STAGE, STAGE):
        if stage < count:
            for copy in copies[2 * stage : 2 * (stage + STAGE)]:
                copy.wait()
        for x in range(stage, stage + STAGE):
            for z in range(2):
                if x < count:
                    multiply(x, z)
                if x >= STAGE:
                    finish(x - STAGE, z)


def edge_of(chip):
    return jnp.where(lax.axis_index("ta") % 2 == 1, chip[:, 0], chip[:, 1]).astype(BF16)


def gather_kernel(received_ref, source_ref, other_ref, chip_ref, edge_ref):
    half = lax.axis_index("ta") % 2

    def summed(first):
        rows = []
        for s in range(2):
            terms = [received_ref[first + s * TSPAN + i] for i in range(TSPAN)]
            rows.append((terms[0] + terms[1]) + (terms[2] + terms[3]))
        return jnp.stack(rows)

    source, other = summed(8 * half), summed(8 - 8 * half)
    chip = jnp.concatenate([source, other], axis=0)
    source_ref[...] = source
    other_ref[...] = other.astype(BF16)
    chip_ref[...] = chip.astype(BF16)
    edge_ref[...] = edge_of(chip)


def forms(v):
    lane = iota((8, WIDE), 1)
    return jnp.concatenate([jnp.where(lane < HALF, v, -v), halves_swapped(v)], axis=0).astype(BF16)


def hops(links_ref, r, z, terms):
    total = None
    for i in range(0, len(terms), 2):
        pair = terms[i : i + 2]
        product = lax.dot_general(
            jnp.concatenate([forms(v) for _, v in pair], axis=1),
            jnp.concatenate([links_ref[d, r, z].reshape(512, WIDE) for d, _ in pair], axis=1),
            (((1,), (1,)), ((), ())),
            preferred_element_type=F32,
        )
        total = product if total is None else total + product
    return total


def applied_here(links_ref, own, other, r):
    rounded = own.astype(BF16).astype(F32)
    low = own - rounded
    plain, lower = [], []
    for z in range(2):
        here = rounded[r, z]
        total = lax.dot_general(
            jnp.concatenate([forms(here), forms(low[r, z])], axis=0),
            links_ref[0, r, z].reshape(512, WIDE),
            (((1,), (1,)), ((), ())),
            preferred_element_type=F32,
        )
        terms = [
            (3, pltpu.roll(here, 7, 0)),
            (4, pltpu.roll(here, 1, 0)),
            (5, rounded[r, 1]) if z == 0 else (6, rounded[r, 0]),
            (7, rounded[1, z] if r == 0 else other[0, z]),
            (8, other[1, z] if r == 0 else rounded[0, z]),
        ]
        plain.append(own_site(total[:16] + hops(links_ref, r, z, terms)))
        lower.append(own_site(total[16:]))
    return jnp.stack(plain), jnp.stack(lower)


def applied_beyond(links_ref, along_x, step_x, along_z, step_z, edge, add):
    for r in range(2):
        for z, terms in (
            (edge, [(step_x, along_x(r, edge)), (step_z, along_z(r))]),
            (1 - edge, [(step_x, along_x(r, 1 - edge))]),
        ):
            add(r, z, own_site(hops(links_ref, r, z, [(d, v.astype(F32)) for d, v in terms])))


def first_here_kernel(links_hbm, source_ref, other_ref, links_ref, plain_ref, lower_ref, links_sem):
    parts = (pl.ds(0, 1), pl.ds(3, 6), pl.ds(1, 2))
    copies = [
        [
            pltpu.make_async_copy(links_hbm.at[part, r], links_ref.at[part, r], links_sem.at[i, r])
            for i, part in enumerate(parts)
        ]
        for r in range(2)
    ]
    for r, i in ((0, 0), (0, 1), (1, 0), (1, 1), (0, 2), (1, 2)):
        copies[r][i].start()
    source, other = source_ref[...], other_ref[...].astype(F32)
    for r in range(2):
        copies[r][0].wait()
        copies[r][1].wait()
        plain_ref[r], lower_ref[r] = applied_here(links_ref, source, other, r)
    copies[0][2].wait()
    copies[1][2].wait()


def near_kernel(links_ref, here_ref, along_x_ref, along_z_ref, _, near_ref):
    odd = lax.axis_index("ta") % 2

    def add(r, z, value):
        near_ref[r, z] = here_ref[r, z] + value

    applied_beyond(
        links_ref, lambda r, z: along_x_ref[r, z], 2 - odd, lambda r: along_z_ref[r], 6 - odd, odd, add
    )


def far(links_ref, near_ref, swapped_ref, total_ref):
    odd = lax.axis_index("ta") % 2

    def add(r, z, value):
        total_ref[r, z] = near_ref[r, z] + value

    applied_beyond(
        links_ref, lambda r, z: swapped_ref[r, z], 1 + odd, lambda r: swapped_ref[r, 2], 5 + odd, 1 - odd, add
    )


def first_far_kernel(links_ref, near_ref, lower_ref, swapped_ref, _, image_ref, full_ref, own_ref):
    far(links_ref, near_ref, swapped_ref, image_ref)
    image = image_ref[...]
    full_ref[...] = image + lower_ref[...]
    own_ref[...] = image.astype(BF16)


def chip_kernel(_, own_ref, other_ref, links_ref, chip_ref, edge_ref):
    chip_ref[:2] = own_ref[...]
    chip_ref[2:] = other_ref[...]
    edge_ref[:4] = edge_of(chip_ref[...].astype(F32))
    edge_ref[4:] = jnp.zeros((EDGE - 4, 8, WIDE), BF16)


def swap_kernel(_, along_x_ref, along_z_ref, links_ref, back_ref):
    back_ref[:, :2] = along_x_ref[2:]
    back_ref[:, 2] = along_z_ref[2:4]


def turned_back(values):
    lane = iota(values.shape, values.ndim - 1)
    swapped = halves_swapped(values)
    return jnp.where(lane < HALF, swapped, -swapped)


def sum_rows(pairs, norms):
    products = []
    for a, b in pairs:
        products += [a * b, a * turned_back(b)]
    products += [a * a for a in norms]
    return [jnp.sum(v.reshape(32, WIDE), axis=0, keepdims=True) for v in products]


def second_here_kernel(links_ref, image_ref, other_ref, source_ref, full_ref, _, here_ref, rows_ref):
    image, other = image_ref[...], other_ref[...].astype(F32)
    for r in range(2):
        plain, lower = applied_here(links_ref, image, other, r)
        here_ref[r] = plain + lower
    source, full = source_ref[...], full_ref[...]
    rows = sum_rows(((image, source), (full, source), (full, image)), (image, full))
    rows_ref[...] = jnp.concatenate(rows, axis=0)


def second_far_kernel(
    links_ref, near_ref, swapped_ref, source_ref, image_ref, full_ref, rows_ref, twice_ref, sums_ref
):
    far(links_ref, near_ref, swapped_ref, twice_ref)
    twice = twice_ref[...]
    rows = sum_rows(((twice, source_ref[...]), (twice, image_ref[...]), (full_ref[...], twice)), (twice,))
    rows = jnp.concatenate([rows_ref[...]] + rows + [jnp.zeros((1, WIDE), F32)], axis=0)
    sums = jnp.sum(rows, axis=1, keepdims=True)
    line = jnp.sum(
        jnp.where(iota((16, WIDE), 0) == iota((16, WIDE), 1), sums, 0.0), axis=0, keepdims=True
    )
    sums_ref[...] = jnp.broadcast_to(line.reshape(1, 1, WIDE), sums_ref.shape)


def last_kernel(sums_ref, source_ref, image_ref, full_ref, twice_ref, solution_ref, residual_ref):
    line = jnp.sum(jnp.sum(sums_ref[...].reshape(16, 8, WIDE), axis=0), axis=0, keepdims=True)

    def at(k):
        return jnp.broadcast_to(line[:, k : k + 1], (8, WIDE))

    def times(a, b):
        return a[0] * b[0] - a[1] * b[1], a[0] * b[1] + a[1] * b[0]

    image_source, full_source, full_image, twice_source, twice_image, full_twice = (
        (at(k), at(k + 1)) for k in (0, 2, 4, 8, 10, 12)
    )
    image_norm, full_norm, twice_norm = at(6), at(7), at(14)
    alpha = image_source[0] / image_norm, image_source[1] / image_norm
    conj = alpha[0], -alpha[1]
    size = alpha[0] * alpha[0] + alpha[1] * alpha[1]
    term_a = times(alpha, full_image)
    term_b = times(conj, twice_source)
    dot = (
        full_source[0] - term_a[0] - term_b[0] + size * twice_image[0],
        full_source[1] - term_a[1] - term_b[1] + size * twice_image[1],
    )
    norm = full_norm - 2.0 * times(alpha, full_twice)[0] + size * twice_norm
    beta = dot[0] / norm, dot[1] / norm

    def scaled(a, values):
        return a[0] * values - a[1] * turned_back(values)

    source = source_ref[...]
    residual = source - scaled(alpha, image_ref[...])
    second = full_ref[...] - scaled(alpha, twice_ref[...])
    solution_ref[...] = scaled(alpha, source) + scaled(beta, residual)
    residual_ref[...] = residual - scaled(beta, second)


def from_core(block):
    return lax.ppermute(block, "ta", [(i, i ^ 1) for i in range(lax.axis_size("ta"))])


def struct(shape, dtype=F32):
    return jax.ShapeDtypeStruct(shape, dtype)


def z_step(block):
    count_ta, count_xyz = lax.axis_size("ta"), lax.axis_size("xyz")
    route = [
        (i * count_xyz + j, i * count_xyz + (j + (1 if i % 2 == 0 else -1)) % count_xyz)
        for i in range(count_ta)
        for j in range(count_xyz)
    ]
    return lax.ppermute(block, ("ta", "xyz"), route)


def x_step(block):
    count = lax.axis_size("ta")
    return lax.ppermute(block, "ta", [(i, (i + (2 if i % 2 == 0 else -2)) % count) for i in range(count)])


def call(kernel, outs, *args, limit=16, aliases=(), scratch=(), specs=None):
    return pl.pallas_call(
        kernel,
        in_specs=specs or [VMEM] * len(args),
        out_specs=[VMEM] * len(outs),
        out_shape=outs,
        input_output_aliases=dict(aliases),
        scratch_shapes=scratch,
        compiler_params=pltpu.CompilerParams(vmem_limit_bytes=limit * MIB),
        name=kernel.__name__,
    )(*args)


def in_hbm(array):
    return pltpu.with_memory_space_constraint(array, pltpu.HBM)


def on_device(fine_field, null_vectors, coarse_links):
    hbm = pl.BlockSpec(memory_space=pltpu.HBM)
    site = (2, 2, 8, WIDE)
    field, coarse = struct(site), struct(site, BF16)
    chip_rows, edge_rows = struct((4, 2, 8, WIDE), BF16), struct((4, 8, WIDE), BF16)
    back_rows = struct((2, 3, 8, WIDE), BF16)
    held = pltpu.VMEM(coarse_links.shape, BF16)
    through = ((0, 0),)

    (send,) = call(
        restrict_kernel,
        [struct((16, 2, 8, WIDE))],
        in_hbm(fine_field),
        in_hbm(null_vectors),
        limit=32,
        specs=[hbm] * 2,
        scratch=[
            pltpu.VMEM(fine_field.shape[1:], BF16),
            pltpu.VMEM(null_vectors.shape[1:], BF16),
            pltpu.VMEM((8, 2, 32, 512), F32),
            pltpu.SemaphoreType.DMA((8,)),
            pltpu.SemaphoreType.DMA((8,)),
        ],
    )
    received = lax.all_to_all(send, "ta", 0, 0)
    source, other, chip, edge = call(gather_kernel, [field, coarse, chip_rows, edge_rows], received)

    along_x, along_z = x_step(chip), z_step(edge)
    links, plain, lower = call(
        first_here_kernel,
        [held, field, field],
        in_hbm(coarse_links),
        source,
        other,
        specs=[hbm, VMEM, VMEM],
        scratch=[pltpu.SemaphoreType.DMA((3, 2))],
    )
    links, back = call(swap_kernel, [held, back_rows], links, along_x, along_z, aliases=through)
    swapped = from_core(back)
    links, near = call(near_kernel, [held, field], links, plain, along_x, along_z, aliases=through)
    links, image, full, own = call(
        first_far_kernel, [held, field, field, coarse], links, near, lower, swapped, aliases=through
    )

    other = from_core(own)
    links, chip, edge = call(chip_kernel, [held, chip_rows, struct((EDGE, 8, WIDE), BF16)], links, own, other, aliases=through)
    along_x, along_z = x_step(chip), z_step(edge)
    links, here, rows = call(
        second_here_kernel, [held, field, struct((8, WIDE))], links, image, other, source, full, aliases=through
    )
    links, back = call(swap_kernel, [held, back_rows], links, along_x, along_z, aliases=through)
    swapped = from_core(back)
    links, near = call(near_kernel, [held, field], links, here, along_x, along_z, aliases=through)
    twice, sums = call(
        second_far_kernel,
        [field, struct((128, 1, WIDE))],
        links,
        near,
        swapped,
        source,
        image,
        full,
        rows,
    )
    sums = lax.all_to_all(sums, ("ta", "xyz"), 0, 0)
    return call(last_kernel, [field, field], sums, source, image, full, twice)


def solution(mesh):
    in_specs = (
        P("ta", None, "xyz", None, None, None),
        P("ta", None, "xyz", None, None, None, None),
        P(None, "ta", "xyz", None, None, None),
    )
    out_specs = (P("ta", "xyz", None, None), P("ta", "xyz", None, None))
    return jax.shard_map(
        on_device, mesh=mesh, in_specs=in_specs, out_specs=out_specs, check_vma=False
    )
```
